32 devices in a mesh: dp: 8 (over z, core), expert: 4 (over y, x).
Axes of the slice: x: 2, y: 2, z: 4, core: 2. Of those that a mesh axis runs over, the one named last changes fastest.
Arguments:
- route_ids: int32 [4096, 2], P(('dp', 'expert')), may hold values from 0 to 3, all different within a row; in each aligned block of 128 rows (0 to 127, 128 to 255, ...) at most 80 rows name the same one
- gate_values: float32 [4096, 2], P(('dp', 'expert')), may hold values from 0.1 to 1
- out_grad: bfloat16 [4096, 2048], P(('dp', 'expert')), may hold values from -4 to 4
- down_weight: bfloat16 [4, 768, 2048], P('expert'), may hold values from -0.21875 to 0.21875
- hidden: bfloat16 [8, 4, 4, 80, 768], P('dp', 'expert'), may hold values from -6 to 6
Outputs:
- mixed_out: bfloat16 [4096, 2048], P(('dp', 'expert'))
- gate_grad: float32 [4096, 2], P(('dp', 'expert'))
- hidden_grad: bfloat16 [8, 4, 4, 80, 768], P('dp', 'expert')
- weight_grad: float32 [4, 768, 2048], P('expert', 'dp')
The draws below stay inside these ranges and needn't reach their ends.
Inputs may be any that keep to these rules, and one draw needn't show every extreme that they name: `route_ids`: each row names 2 different experts. Among the rows of one device no expert is named by more than 80 rows, and in every draw some device names some expert exactly 80 times.
All inputs are finite; a program needn't handle non-finite values.
Results may differ from the reference program's by a relative error of at most 0.0049.
Values may be sent and summed in bfloat16 or wider, within the bound.
A program may use at most 64 MiB of HBM per device.

```python
import math
import jax
import jax.numpy as jnp
import numpy as np
from jax import lax

D_W = 2048
H = 768
TOP = 2
TOK_DEV = 128
EXPERTS = 4
CAP = 80
TOKENS = 4096
N_DP = 8
N_EXPERT = 4


def spiked(values, stream_key, source, target, blocks, factor):
    def block_of(position):
        return (jnp.arange(values.shape[position]) // (values.shape[position] // blocks)).reshape((-1,) + (1,) * (values.ndim - 1 - position))

    first = jax.random.permutation(stream_key, blocks)[block_of(target)]
    other_side = (block_of(target) + blocks // 2) % blocks
    return jnp.where((block_of(source) == first) | (block_of(source) == other_side), factor * values, values)


def block_levels(key, shape, cuts, low, top_value):
    level, own = 1.0, jax.random.fold_in(key, 6)
    for dim, shards_of in cuts:
        steps = jnp.exp(jax.random.uniform(jax.random.fold_in(own, dim), (shards_of,), jnp.float32, low / len(cuts), top_value / len(cuts)))
        level = level * jnp.repeat(steps, shape[dim] // shards_of).reshape([-1 if axis == dim else 1 for axis in range(len(shape))])
    return level


def shared_out(own_key, own, number, rows, count, top, limit, lean):
    ranking = jax.random.permutation(own_key, count)
    heavy_load, common = portions_of(count, rows * top, limit, lean, True), portions_of(count, rows * top, limit, lean, False)
    places = jnp.arange(count)

    def named(lengths, offset_by):
        used = int((lengths > 0).sum())
        fixed = max(1, used // 4)
        moved = fixed + (places - fixed + offset_by * (used - fixed)) % max(1, count - fixed)
        return jnp.zeros((count,), jnp.int32).at[ranking[jnp.where(places < fixed, places, moved)]].set(jnp.asarray(lengths, jnp.int32))

    lengths = jnp.where(number % 4 == 0, named(heavy_load, number // 4), named(common, number - number // 4 - 1))
    mixed = jax.random.permutation(jax.random.fold_in(own, 3), count)
    donor, receiver = mixed[0:count // 2 * 2:2], mixed[1:count // 2 * 2:2]
    margin = jnp.minimum(lengths[donor] - 1, limit - lengths[receiver]) // 2
    margin = jnp.where((donor == ranking[0]) | (receiver == ranking[0]) | (lengths[receiver] == 0), 0, jnp.maximum(margin, 0))
    moved = jax.random.randint(jax.random.fold_in(own, 4), (count // 2,), 0, 1 << 20) % (margin + 1)
    lengths = lengths.at[donor].add(-moved).at[receiver].add(moved)
    members = jnp.searchsorted(jnp.cumsum(lengths), jnp.arange(rows * top), side="right").astype(jnp.int32)
    grid = members.reshape(top, rows).T
    grid = grid[jax.random.permutation(jax.random.fold_in(own, 1), rows)]
    offset_by = jax.random.randint(jax.random.fold_in(own, 2), (rows, 1), 0, top)
    return jnp.take_along_axis(grid, (jnp.arange(top)[None, :] + offset_by) % top, axis=1)


def portions_of(number_of, total, bound, lean, full):
    weights = [(1 << 20) // math.isqrt(grade ** lean) + 1 for grade in range(1, number_of + 1)]
    largest = bound if full else min(bound, max(-(-total // number_of), total * weights[0] // sum(weights)))
    least = 1 if total - largest >= number_of - 1 else 0
    holding, surplus = [largest] + [least] * (number_of - 1), total - largest - least * (number_of - 1)
    while surplus > 0:
        movable = [i for i in range(1, number_of) if holding[i] < largest] or [i for i in range(1, number_of) if holding[i] < bound]
        whole, left = sum([weights[i] for i in movable]), surplus
        for i in movable:
            extra = min(bound - holding[i], max(1, left * weights[i] // whole), surplus)
            holding[i] = holding[i] + extra
            surplus = surplus - extra
    return np.array(holding)


def bell_draw(rng, dims, scale, reach, pieces=(), held_as=jnp.bfloat16):
    entries = jax.random.normal(rng, dims, jnp.float32) * scale
    if len(pieces) > 0:
        entries = block_levels(rng, dims, pieces, -0.22, 0.18) * entries
    return jnp.clip(entries, min=-reach, max=reach).astype(held_as)


def gaussian_with(key, extent, width, most, shards, heavy, held_as=jnp.bfloat16):
    array = width * jax.random.normal(key, extent, jnp.float32)
    if shards:
        array = array * block_levels(key, extent, shards, -0.22, 0.18)
    return jnp.clip(spiked(array, jax.random.fold_in(key, 3), *heavy), -most, most).astype(held_as)


def setup_inputs(seed: int = 0) -> dict:
    key_of = jax.random.split(jax.random.key(seed), 6)
    route_ids_keys = jax.random.split(jax.random.fold_in(key_of[0], 1), TOKENS // TOK_DEV)
    route_ids_turns = jax.random.permutation(jax.random.fold_in(key_of[0], 3), TOKENS // TOK_DEV)
    route_ids = jax.vmap(lambda own, number: shared_out(jax.random.fold_in(key_of[0], 2), own, number, TOK_DEV, EXPERTS, TOP, CAP, 2))(route_ids_keys, route_ids_turns).reshape((TOKENS, TOP))
    gate_values = jnp.clip(jnp.exp(math.log(1.0) - 2.3025851 * jax.random.uniform(key_of[1], (TOKENS, TOP), jnp.float32) ** block_levels(key_of[1], (TOKENS, TOP), ((0, 32),), -0.2, 0.2)), 0.1, 1.0)
    out_grad = bell_draw(key_of[2], (TOKENS, D_W), 0.25, 4.0, ((0, 32),))
    down_weight = bell_draw(key_of[3], (EXPERTS, H, D_W), H ** -0.5, 0.21875, ((0, 4),))
    hidden = gaussian_with(key_of[4], (N_DP, EXPERTS, N_EXPERT, CAP, H), 1.0, 6.0, ((0, 8), (1, 4)), (0, 4, 8, 2.0))
    return dict(route_ids=route_ids, gate_values=gate_values, out_grad=out_grad, down_weight=down_weight, hidden=hidden)


def slot_table(route_ids, experts, capacity):
    flat_ids = route_ids.reshape(-1)
    route_count = flat_ids.shape[0]
    onehot = (flat_ids[:, None] == jnp.arange(experts, dtype=jnp.int32)[None, :]).astype(jnp.float32)
    positions = jnp.arange(route_count, dtype=jnp.int32)
    earlier = (positions[:, None] > positions[None, :]).astype(jnp.float32)
    before = jnp.dot(earlier, onehot, precision=lax.Precision.HIGHEST, preferred_element_type=jnp.float32)
    slot_rank = jnp.sum(before * onehot, axis=1).astype(jnp.int32)
    slot_index = flat_ids * capacity + slot_rank
    slots_all = jnp.arange(experts * capacity, dtype=jnp.int32)
    return (slots_all[:, None] == slot_index[None, :]).astype(jnp.float32)


def reference(route_ids, gate_values, out_grad, down_weight, hidden):
    ids_all = route_ids.reshape(N_DP, N_EXPERT, TOK_DEV, TOP)
    gates_all = gate_values.reshape(N_DP, N_EXPERT, TOK_DEV, TOP)
    grads_all = out_grad.reshape(N_DP, N_EXPERT, TOK_DEV, D_W)
    weight_f = down_weight.astype(jnp.float32)

    def one_source(ids_one, gates_one, grads_one, outs_one):
        slot_map = slot_table(ids_one, EXPERTS, CAP)
        rows_back = outs_one.reshape(EXPERTS * CAP, D_W).astype(jnp.float32)
        routed = jnp.dot(slot_map.T, rows_back, precision=lax.Precision.HIGHEST, preferred_element_type=jnp.float32)
        routed = routed.reshape(TOK_DEV, TOP, D_W)
        grads_f = grads_one.astype(jnp.float32)
        mixed_one = jnp.sum(gates_one[:, :, None] * routed, axis=1).astype(jnp.bfloat16)
        gate_one = jnp.sum(routed * grads_f[:, None, :], axis=2)
        scaled = (gates_one[:, :, None] * grads_f[:, None, :]).reshape(TOK_DEV * TOP, D_W).astype(jnp.bfloat16)
        outgoing = jnp.dot(slot_map, scaled.astype(jnp.float32), precision=lax.Precision.HIGHEST, preferred_element_type=jnp.float32)
        outgoing = outgoing.astype(jnp.bfloat16).reshape(EXPERTS, CAP, D_W)
        return mixed_one, gate_one, outgoing

    def per_group(total_grad, inputs):
        ids_grp, gates_grp, grads_grp, hidden_grp = inputs
        hidden_f = hidden_grp.astype(jnp.float32)
        expert_out = jnp.einsum("esch,ehd->escd", hidden_f, weight_f).astype(jnp.bfloat16)
        by_source = jnp.transpose(expert_out, (1, 0, 2, 3))
        mixed_grp, gate_grp, sent = jax.vmap(one_source)(ids_grp, gates_grp, grads_grp, by_source)
        expert_grad = jnp.transpose(sent, (1, 0, 2, 3)).astype(jnp.float32)
        hidden_grad = jnp.einsum("escd,ehd->esch", expert_grad, weight_f).astype(jnp.bfloat16)
        partial_term = jnp.einsum("esch,escd->ehd", hidden_f, expert_grad)
        return total_grad + partial_term, (mixed_grp, gate_grp, hidden_grad)

    start_grad = jnp.zeros((EXPERTS, H, D_W), jnp.float32)
    weight_grad, (mixed_all, gate_all, hidden_grad) = lax.scan(per_group, start_grad, (ids_all, gates_all, grads_all, hidden))
    return (mixed_all.reshape(TOKENS, D_W), gate_all.reshape(TOKENS, TOP), hidden_grad, weight_grad)
```

```python
import functools

import jax
import jax.numpy as jnp
from jax import lax
from jax.experimental import pallas as pl
from jax.experimental.pallas import tpu as pltpu
from jax.sharding import PartitionSpec as P


MESH = pl.DeviceIdType.MESH
CHUNKS = 8
F32 = jnp.float32
BF16 = jnp.bfloat16


def slot_table(route_ids, experts, capacity):
    flat_ids = route_ids.reshape(-1)
    route_count = flat_ids.shape[0]
    onehot = (flat_ids[:, None] == jnp.arange(experts, dtype=jnp.int32)[None, :]).astype(
        jnp.float32
    )
    positions = jnp.arange(route_count, dtype=jnp.int32)
    earlier = (positions[:, None] > positions[None, :]).astype(jnp.float32)
    before = jnp.dot(
        earlier, onehot, precision=lax.Precision.HIGHEST, preferred_element_type=jnp.float32
    )
    slot_rank = jnp.sum(before * onehot, axis=1).astype(jnp.int32)
    slot_index = flat_ids * capacity + slot_rank
    slots_all = jnp.arange(experts * capacity, dtype=jnp.int32)
    return (slots_all[:, None] == slot_index[None, :]).astype(jnp.bfloat16)


def on_device_generic(route_ids, gate_values, out_grad, down_weight, hidden):
    experts = lax.axis_size("expert")
    capacity = hidden.shape[3]
    inner_width = hidden.shape[4]
    feature_width = out_grad.shape[1]
    tok_rows = route_ids.shape[0]
    routes = route_ids.shape[1]
    slot_map = slot_table(route_ids, experts, capacity)
    weight_mat = down_weight[0]
    rows_in = hidden.reshape(-1, inner_width)
    expert_out = jnp.dot(rows_in, weight_mat, preferred_element_type=jnp.float32)
    expert_out = expert_out.astype(jnp.bfloat16).reshape(experts, capacity, feature_width)
    grads_f = out_grad.astype(jnp.float32)
    scaled = (
        (gate_values[:, :, None] * grads_f[:, None, :])
        .reshape(-1, feature_width)
        .astype(jnp.bfloat16)
    )
    outgoing = jnp.dot(slot_map, scaled, preferred_element_type=jnp.float32)
    outgoing = outgoing.astype(jnp.bfloat16).reshape(experts, capacity, feature_width)
    returned = lax.all_to_all(expert_out, "expert", split_axis=0, concat_axis=0, tiled=True)
    incoming = lax.all_to_all(outgoing, "expert", split_axis=0, concat_axis=0, tiled=True)
    gathered = jnp.einsum(
        "sr,sd->rd",
        slot_map,
        returned.reshape(-1, feature_width),
        preferred_element_type=jnp.float32,
    )
    gathered = gathered.reshape(tok_rows, routes, feature_width)
    mixed_out = jnp.sum(gate_values[:, :, None] * gathered, axis=1).astype(jnp.bfloat16)
    gate_grad = jnp.sum(gathered * grads_f[:, None, :], axis=2)
    grad_rows = incoming.reshape(-1, feature_width)
    hidden_grad = jnp.einsum("sd,hd->sh", grad_rows, weight_mat, preferred_element_type=jnp.float32)
    hidden_grad = hidden_grad.astype(jnp.bfloat16).reshape(hidden.shape)
    partial_term = jnp.einsum("sh,sd->hd", rows_in, grad_rows, preferred_element_type=jnp.float32)
    weight_grad = lax.psum_scatter(partial_term, "dp", scatter_dimension=0, tiled=True)
    return (mixed_out, gate_grad, hidden_grad, weight_grad[None])


def fused_kernel(
    nf, ids_ref, gates_ref, og_ref, w_ref, hid_ref,
    mixed_ref, gate_ref, hg_ref, wg_ref,
    hall, ht, sel, sel_t, gslot, gcol, outg, inc, eo, ret, csend, crecv, acc,
    rsend, rrecv, lsend, lrecv, hgacc, qacc,
    cot_s, cot_r, eo_s, eo_r, core_s, core_r, rs, rr, ls, lr,
):
    dp, me = lax.axis_index("dp"), lax.axis_index("expert")
    ne = lax.axis_size("expert")
    nz = lax.axis_size("dp") // 2
    z, core = lax.div(dp, 2), lax.rem(dp, 2)
    tok, top = ids_ref.shape
    cap = inc.shape[2]
    fc = inc.shape[3]
    width = hid_ref.shape[1]
    block = wg_ref.shape[0]
    slots = ne * cap
    mate = 2 * z + 1 - core

    barrier = pltpu.get_barrier_semaphore()
    for d in range(1, ne):
        pl.semaphore_signal(barrier, inc=1, device_id=(dp, lax.rem(me + d, ne)), device_id_type=MESH)
    pl.semaphore_signal(barrier, inc=1, device_id=(mate, me), device_id_type=MESH)

    @pl.when(z > 0)
    def _():
        pl.semaphore_signal(barrier, inc=1, device_id=(dp - 2, me), device_id_type=MESH)

    @pl.when(z < nz - 1)
    def _():
        pl.semaphore_signal(barrier, inc=1, device_id=(dp + 2, me), device_id_type=MESH)

    ids = ids_ref[...]
    gates = gates_ref[...]
    row = lax.broadcasted_iota(jnp.int32, (tok, tok), 0)
    col = lax.broadcasted_iota(jnp.int32, (tok, tok), 1)
    diagonal = row == col
    earlier = col < row
    slot_rows = lax.broadcasted_iota(jnp.int32, (cap, tok), 0).astype(F32)
    slot_cols = lax.broadcasted_iota(jnp.int32, (tok, cap), 1).astype(F32)

    def to_row(column):
        return jnp.sum(jnp.where(diagonal, column, 0.0), axis=0, keepdims=True)

    for e in range(ne):
        named = jnp.sum(jnp.where(ids == e, 1.0, 0.0), axis=1, keepdims=True)
        gate = jnp.sum(jnp.where(ids == e, gates, 0.0), axis=1, keepdims=True)
        rank = jnp.sum(jnp.where(earlier, to_row(named), 0.0), axis=1, keepdims=True)
        place = jnp.where(named > 0.0, rank, -1.0)
        hit = slot_rows == to_row(place)
        sel[e] = jnp.where(hit, 1.0, 0.0).astype(BF16)
        gslot[e] = jnp.sum(jnp.where(hit, to_row(gate), 0.0), axis=1, keepdims=True)
        sel_t[e] = jnp.where(slot_cols == place, 1.0, 0.0).astype(BF16)
        gcol[e] = gate

    count = ne + jnp.where(z > 0, 1, 0) + jnp.where(z < nz - 1, 1, 0)
    pl.semaphore_wait(barrier, count)

    def columns(f):
        return pl.ds(pl.multiple_of(f * fc, fc), fc)

    def cot_copy(f, d, peer, slot):
        return pltpu.make_async_remote_copy(
            src_ref=outg.at[f, d - 1], dst_ref=inc.at[f, slot],
            send_sem=cot_s.at[f, d - 1], recv_sem=cot_r.at[f, d - 1],
            device_id=(dp, peer), device_id_type=MESH)

    def eo_copy(f, d, peer, slot):
        return pltpu.make_async_remote_copy(
            src_ref=eo.at[f, peer], dst_ref=ret.at[f, slot],
            send_sem=eo_s.at[f, d - 1], recv_sem=eo_r.at[f, d - 1],
            device_id=(dp, peer), device_id_type=MESH)

    def core_copy(f):
        return pltpu.make_async_remote_copy(
            src_ref=csend.at[f], dst_ref=crecv.at[f],
            send_sem=core_s.at[f], recv_sem=core_r.at[f],
            device_id=(mate, me), device_id_type=MESH)

    def up_copy(f, zz):
        return pltpu.make_async_remote_copy(
            src_ref=rsend.at[f, zz], dst_ref=rrecv.at[f, zz],
            send_sem=rs.at[f, zz], recv_sem=rr.at[f, zz],
            device_id=(lax.rem(dp + 2, 2 * nz), me), device_id_type=MESH)

    def down_copy(f, zz):
        return pltpu.make_async_remote_copy(
            src_ref=lsend.at[f, zz], dst_ref=lrecv.at[f, zz],
            send_sem=ls.at[f, zz], recv_sem=lr.at[f, zz],
            device_id=(lax.rem(dp + 2 * nz - 2, 2 * nz), me), device_id_type=MESH)

    @pl.loop(0, nf)
    def _(f):
        grads = og_ref[:, columns(f)]
        for d in (*range(1, ne), 0):
            e = lax.rem(me + d, ne)
            rows = jnp.dot(sel[e], grads, preferred_element_type=F32)
            rows = (gslot[e] * rows).astype(BF16)
            if d:
                outg[f, d - 1] = rows
                cot_copy(f, d, e, me).start()
            else:
                inc[f, me] = rows

    hall[...] = hid_ref[...].T
    for zz in range(nz):
        ht[0, zz] = hall[pl.ds(pl.multiple_of(block * (2 * zz + 1 - core), block), block), :]
        ht[1, zz] = hall[pl.ds(pl.multiple_of(block * (2 * zz + core), block), block), :]
    hgacc[...] = jnp.zeros_like(hgacc)
    qacc[...] = jnp.zeros_like(qacc)

    @pl.loop(0, nf + nz - 1)
    def _(s):
        @pl.when(s < nf)
        def _():
            f = s
            weight = w_ref[:, columns(f)]
            y = jnp.dot(hid_ref[...], weight, preferred_element_type=F32)
            eo[f] = y.astype(BF16).reshape(ne, cap, fc)
            for d in range(1, ne):
                e = lax.rem(me + ne - d, ne)
                cot_copy(f, d, e, e).wait_recv()
            x = inc[f].reshape(slots, fc)
            other = jnp.dot(ht[0].reshape(nz * block, slots), x, preferred_element_type=F32)
            csend[f] = other.astype(BF16).reshape(nz, block, fc)
            core_copy(f).start()
            for d in range(1, ne):
                e = lax.rem(me + d, ne)
                eo_copy(f, d, e, me).start()
            ret[f, me] = eo[f, me]
            own = jnp.dot(ht[1].reshape(nz * block, slots), x, preferred_element_type=F32)
            acc[f] = own.reshape(nz, block, fc)
            hgacc[...] += lax.dot_general(
                x, weight, (((1,), (1,)), ((), ())), preferred_element_type=F32)
            core_copy(f).wait_recv()
            acc[f] += crecv[f].astype(F32)

        up = s - z

        @pl.when((up >= 0) & (up < nf))
        def _():
            for zz in range(nz - 1, 0, -1):
                @pl.when((zz > z) & (z > 0))
                def _():
                    up_copy(up, zz).wait_recv()
                    rsend[up, zz] = (acc[up, zz] + rrecv[up, zz].astype(F32)).astype(BF16)
                    up_copy(up, zz).start()

                @pl.when((zz > z) & (z == 0))
                def _():
                    rsend[up, zz] = acc[up, zz].astype(BF16)
                    up_copy(up, zz).start()

        down = s - (nz - 1 - z)

        @pl.when((down >= 0) & (down < nf))
        def _():
            for zz in range(nz - 1):
                @pl.when((zz < z) & (z < nz - 1))
                def _():
                    down_copy(down, zz).wait_recv()
                    lsend[down, zz] = (acc[down, zz] + lrecv[down, zz].astype(F32)).astype(BF16)
                    down_copy(down, zz).start()

                @pl.when((zz < z) & (z == nz - 1))
                def _():
                    lsend[down, zz] = acc[down, zz].astype(BF16)
                    down_copy(down, zz).start()

        back = s - (nz - 1)

        @pl.when(back >= 0)
        def _():
            f = back
            for d in range(1, ne):
                e = lax.rem(me + ne - d, ne)
                eo_copy(f, d, e, e).wait_recv()
            grads = og_ref[:, columns(f)].astype(F32)
            mixed = jnp.zeros((tok, fc), F32)
            for e in range(ne):
                routed = jnp.dot(sel_t[e], ret[f, e], preferred_element_type=F32)
                mixed += gcol[e] * routed
                product = routed * grads
                part = product[:, 0:128]
                for j in range(128, fc, 128):
                    part += product[:, j:j + 128]
                qacc[e] += part
            mixed_ref[:, columns(f)] = mixed.astype(BF16)

            wg_ref[:, columns(f)] = acc[f, z]

            @pl.when(z > 0)
            def _():
                up_copy(f, z).wait_recv()
                wg_ref[:, columns(f)] += rrecv[f, z].astype(F32)

            @pl.when(z < nz - 1)
            def _():
                down_copy(f, z).wait_recv()
                wg_ref[:, columns(f)] += lrecv[f, z].astype(F32)

    hg_ref[...] = hgacc[...].astype(BF16)
    parts = []
    for k in range(top):
        total = jnp.zeros((tok, 1), F32)
        for e in range(ne):
            total += jnp.where(ids[:, k:k + 1] == e, jnp.sum(qacc[e], axis=1, keepdims=True), 0.0)
        parts.append(total)
    for k in range(top):
        gate_ref[:, k:k + 1] = parts[k]

    @pl.loop(0, nf)
    def _(f):
        core_copy(f).wait_send()
        for d in range(1, ne):
            e = lax.rem(me + d, ne)
            cot_copy(f, d, e, me).wait_send()
            eo_copy(f, d, e, me).wait_send()
        for zz in range(nz):
            @pl.when(zz > z)
            def _():
                up_copy(f, zz).wait_send()

            @pl.when(zz < z)
            def _():
                down_copy(f, zz).wait_send()


def on_device(route_ids, gate_values, out_grad, down_weight, hidden):
    ne = lax.axis_size("expert")
    nz = lax.axis_size("dp") // 2
    cap, width = hidden.shape[3:]
    tok, feat = out_grad.shape
    top = route_ids.shape[1]
    nf = CHUNKS
    fc = feat // nf
    block = width // (2 * nz)
    slots = ne * cap
    chain = pltpu.VMEM((nf, nz, block, fc), BF16)
    dma = pltpu.SemaphoreType.DMA
    vmem = pl.BlockSpec(memory_space=pltpu.VMEM)
    mixed, gate, hg, wg = pl.pallas_call(
        functools.partial(fused_kernel, nf),
        out_shape=(
            jax.ShapeDtypeStruct((tok, feat), BF16),
            jax.ShapeDtypeStruct((tok, top), F32),
            jax.ShapeDtypeStruct((slots, width), BF16),
            jax.ShapeDtypeStruct((block, feat), F32),
        ),
        in_specs=[vmem] * 5,
        out_specs=(vmem,) * 4,
        scratch_shapes=[
            pltpu.VMEM((width, slots), BF16),
            pltpu.VMEM((2, nz, block, slots), BF16),
            pltpu.VMEM((ne, cap, tok), BF16),
            pltpu.VMEM((ne, tok, cap), BF16),
            pltpu.VMEM((ne, cap, 1), F32),
            pltpu.VMEM((ne, tok, 1), F32),
            pltpu.VMEM((nf, ne - 1, cap, fc), BF16),
            pltpu.VMEM((nf, ne, cap, fc), BF16),
            pltpu.VMEM((nf, ne, cap, fc), BF16),
            pltpu.VMEM((nf, ne, cap, fc), BF16),
            chain,
            chain,
            pltpu.VMEM((nf, nz, block, fc), F32),
            chain,
            chain,
            chain,
            chain,
            pltpu.VMEM((slots, width), F32),
            pltpu.VMEM((ne, tok, 128), F32),
            dma((nf, ne - 1)),
            dma((nf, ne - 1)),
            dma((nf, ne - 1)),
            dma((nf, ne - 1)),
            dma((nf,)),
            dma((nf,)),
            dma((nf, nz)),
            dma((nf, nz)),
            dma((nf, nz)),
            dma((nf, nz)),
        ],
        compiler_params=pltpu.CompilerParams(
            collective_id=0, has_side_effects=True, vmem_limit_bytes=52 * 1024 * 1024
        ),
        cost_estimate=pl.CostEstimate(
            flops=6 * slots * width * feat, bytes_accessed=2 * width * feat, transcendentals=0
        ),
    )(route_ids, gate_values, out_grad, down_weight[0], hidden.reshape(slots, width))
    return mixed, gate, hg.reshape(hidden.shape), wg[None]


def fits(mesh):
    return mesh.shape["expert"] <= 4 and mesh.shape["dp"] in (2, 4, 8)


def solution(mesh):
    in_specs = (
        P(("dp", "expert"), None),
        P(("dp", "expert"), None),
        P(("dp", "expert"), None),
        P("expert", None, None),
        P("dp", "expert", None, None, None),
    )
    out_specs = (
        P(("dp", "expert"), None),
        P(("dp", "expert"), None),
        P("dp", "expert", None, None, None),
        P("expert", "dp", None),
    )
    body = on_device if fits(mesh) else on_device_generic
    return jax.shard_map(
        body, mesh=mesh, in_specs=in_specs, out_specs=out_specs, check_vma=False
    )
```

```python
import functools

import jax
import jax.numpy as jnp
from jax import lax
from jax.experimental import pallas as pl
from jax.experimental.pallas import tpu as pltpu
from jax.sharding import PartitionSpec as P


MESH = pl.DeviceIdType.MESH
CHUNKS = 8
AHEAD = 2
F32 = jnp.float32
BF16 = jnp.bfloat16


def slot_table(route_ids, experts, capacity):
    flat_ids = route_ids.reshape(-1)
    route_count = flat_ids.shape[0]
    onehot = (flat_ids[:, None] == jnp.arange(experts, dtype=jnp.int32)[None, :]).astype(
        jnp.float32
    )
    positions = jnp.arange(route_count, dtype=jnp.int32)
    earlier = (positions[:, None] > positions[None, :]).astype(jnp.float32)
    before = jnp.dot(
        earlier, onehot, precision=lax.Precision.HIGHEST, preferred_element_type=jnp.float32
    )
    slot_rank = jnp.sum(before * onehot, axis=1).astype(jnp.int32)
    slot_index = flat_ids * capacity + slot_rank
    slots_all = jnp.arange(experts * capacity, dtype=jnp.int32)
    return (slots_all[:, None] == slot_index[None, :]).astype(jnp.bfloat16)


def on_device_generic(route_ids, gate_values, out_grad, down_weight, hidden):
    experts = lax.axis_size("expert")
    capacity = hidden.shape[3]
    inner_width = hidden.shape[4]
    feature_width = out_grad.shape[1]
    tok_rows = route_ids.shape[0]
    routes = route_ids.shape[1]
    slot_map = slot_table(route_ids, experts, capacity)
    weight_mat = down_weight[0]
    rows_in = hidden.reshape(-1, inner_width)
    expert_out = jnp.dot(rows_in, weight_mat, preferred_element_type=jnp.float32)
    expert_out = expert_out.astype(jnp.bfloat16).reshape(experts, capacity, feature_width)
    grads_f = out_grad.astype(jnp.float32)
    scaled = (
        (gate_values[:, :, None] * grads_f[:, None, :])
        .reshape(-1, feature_width)
        .astype(jnp.bfloat16)
    )
    outgoing = jnp.dot(slot_map, scaled, preferred_element_type=jnp.float32)
    outgoing = outgoing.astype(jnp.bfloat16).reshape(experts, capacity, feature_width)
    returned = lax.all_to_all(expert_out, "expert", split_axis=0, concat_axis=0, tiled=True)
    incoming = lax.all_to_all(outgoing, "expert", split_axis=0, concat_axis=0, tiled=True)
    gathered = jnp.einsum(
        "sr,sd->rd",
        slot_map,
        returned.reshape(-1, feature_width),
        preferred_element_type=jnp.float32,
    )
    gathered = gathered.reshape(tok_rows, routes, feature_width)
    mixed_out = jnp.sum(gate_values[:, :, None] * gathered, axis=1).astype(jnp.bfloat16)
    gate_grad = jnp.sum(gathered * grads_f[:, None, :], axis=2)
    grad_rows = incoming.reshape(-1, feature_width)
    hidden_grad = jnp.einsum("sd,hd->sh", grad_rows, weight_mat, preferred_element_type=jnp.float32)
    hidden_grad = hidden_grad.astype(jnp.bfloat16).reshape(hidden.shape)
    partial_term = jnp.einsum("sh,sd->hd", rows_in, grad_rows, preferred_element_type=jnp.float32)
    weight_grad = lax.psum_scatter(partial_term, "dp", scatter_dimension=0, tiled=True)
    return (mixed_out, gate_grad, hidden_grad, weight_grad[None])


def fused_kernel(
    nf, ids_ref, gates_ref, og_hbm, w_hbm, hid_hbm,
    mixed_ref, gate_ref, hg_ref, wg_ref,
    og, wt, hid, hall, ht, sel, sel_t, gslot, gcol, outg, inc, eo, ret, csend, crecv, acc,
    rsend, rrecv, lsend, lrecv, hgacc, qacc,
    cot_s, cot_r, eo_s, eo_r, core_s, core_r, rs, rr, ls, lr, load,
):
    dp, me = lax.axis_index("dp"), lax.axis_index("expert")
    ne = lax.axis_size("expert")
    nz = lax.axis_size("dp") // 2
    z, core = lax.div(dp, 2), lax.rem(dp, 2)
    top, tok = ids_ref.shape
    cap = inc.shape[2]
    fc = inc.shape[3]
    block = wg_ref.shape[0]
    slots = ne * cap
    mate = 2 * z + 1 - core

    loads = [
        pltpu.make_async_copy(src, dst, load.at[i])
        for i, (src, dst) in enumerate(((og_hbm, og), (hid_hbm, hid), (w_hbm, wt)))
    ]
    for copy in loads:
        copy.start()

    barrier = pltpu.get_barrier_semaphore()
    for d in range(1, ne):
        pl.semaphore_signal(barrier, inc=1, device_id=(dp, lax.rem(me + d, ne)), device_id_type=MESH)
    pl.semaphore_signal(barrier, inc=1, device_id=(mate, me), device_id_type=MESH)

    @pl.when(z > 0)
    def _():
        pl.semaphore_signal(barrier, inc=1, device_id=(dp - 2, me), device_id_type=MESH)

    @pl.when(z < nz - 1)
    def _():
        pl.semaphore_signal(barrier, inc=1, device_id=(dp + 2, me), device_id_type=MESH)

    ids = ids_ref[...]
    gates = gates_ref[...]
    row = lax.broadcasted_iota(jnp.int32, (tok, tok), 0)
    col = lax.broadcasted_iota(jnp.int32, (tok, tok), 1)
    diagonal = row == col
    earlier = row < col
    slot_rows = lax.broadcasted_iota(jnp.int32, (cap, tok), 0).astype(F32)
    slot_cols = lax.broadcasted_iota(jnp.int32, (tok, cap), 1).astype(F32)

    def to_column(values):
        return jnp.sum(jnp.where(diagonal, values, 0.0), axis=1, keepdims=True)

    def to_row(values):
        return jnp.sum(jnp.where(diagonal, values, 0.0), axis=0, keepdims=True)

    for e in range(ne):
        named = jnp.sum(jnp.where(ids == e, 1.0, 0.0), axis=0, keepdims=True)
        gate = jnp.sum(jnp.where(ids == e, gates, 0.0), axis=0, keepdims=True)
        rank = jnp.sum(jnp.where(earlier, to_column(named), 0.0), axis=0, keepdims=True)
        place = jnp.where(named > 0.0, rank, -1.0)
        hit = slot_rows == place
        sel[e] = jnp.where(hit, 1.0, 0.0).astype(BF16)
        gslot[e] = jnp.sum(jnp.where(hit, gate, 0.0), axis=1, keepdims=True)
        sel_t[e] = jnp.where(slot_cols == to_column(place), 1.0, 0.0).astype(BF16)
        gcol[e] = to_column(gate)

    count = ne + jnp.where(z > 0, 1, 0) + jnp.where(z < nz - 1, 1, 0)
    pl.semaphore_wait(barrier, count)

    def columns(f):
        return pl.ds(pl.multiple_of(f * fc, fc), fc)

    def cot_copy(f, d, peer, slot):
        return pltpu.make_async_remote_copy(
            src_ref=outg.at[f, d - 1], dst_ref=inc.at[f, slot],
            send_sem=cot_s.at[f, d - 1], recv_sem=cot_r.at[f, d - 1],
            device_id=(dp, peer), device_id_type=MESH)

    def eo_copy(f, d, peer, slot):
        return pltpu.make_async_remote_copy(
            src_ref=eo.at[f, peer], dst_ref=ret.at[f, slot],
            send_sem=eo_s.at[f, d - 1], recv_sem=eo_r.at[f, d - 1],
            device_id=(dp, peer), device_id_type=MESH)

    def core_copy(f):
        return pltpu.make_async_remote_copy(
            src_ref=csend.at[f], dst_ref=crecv.at[f],
            send_sem=core_s.at[f], recv_sem=core_r.at[f],
            device_id=(mate, me), device_id_type=MESH)

    def up_copy(f, k):
        return pltpu.make_async_remote_copy(
            src_ref=rsend.at[f, k], dst_ref=rrecv.at[f, k],
            send_sem=rs.at[f, k], recv_sem=rr.at[f, k],
            device_id=(lax.rem(dp + 2, 2 * nz), me), device_id_type=MESH)

    def down_copy(f, k):
        return pltpu.make_async_remote_copy(
            src_ref=lsend.at[f, k], dst_ref=lrecv.at[f, k],
            send_sem=ls.at[f, k], recv_sem=lr.at[f, k],
            device_id=(lax.rem(dp + 2 * nz - 2, 2 * nz), me), device_id_type=MESH)

    def send_cotangents(f):
        grads = og[:, columns(f)]
        for d in (*range(1, ne), 0):
            e = lax.rem(me + d, ne)
            rows = jnp.dot(sel[e], grads, preferred_element_type=F32)
            rows = (gslot[e] * rows).astype(BF16)
            if d:
                outg[f, d - 1] = rows
                cot_copy(f, d, e, me).start()
            else:
                inc[f, me] = rows

    loads[0].wait()

    @pl.loop(0, AHEAD)
    def _(f):
        send_cotangents(f)

    loads[1].wait()
    hall[...] = hid[...].T
    for zz in range(nz):
        ht[0, zz] = hall[pl.ds(pl.multiple_of(block * (2 * zz + 1 - core), block), block), :]
        ht[1, zz] = hall[pl.ds(pl.multiple_of(block * (2 * zz + core), block), block), :]
    loads[2].wait()
    hgacc[...] = jnp.zeros_like(hgacc)
    qacc[...] = jnp.zeros_like(qacc)

    @pl.loop(0, nf + nz - 1)
    def _(s):
        @pl.when(s < nf)
        def _():
            f = s

            @pl.when(f + AHEAD < nf)
            def _():
                send_cotangents(f + AHEAD)

            for d in range(1, ne):
                e = lax.rem(me + ne - d, ne)
                cot_copy(f, d, e, e).wait_recv()
            x = inc[f].reshape(slots, fc)
            other = jnp.dot(ht[0].reshape(nz * block, slots), x, preferred_element_type=F32)
            csend[f] = other.astype(BF16).reshape(nz, block, fc)
            core_copy(f).start()
            own = jnp.dot(ht[1].reshape(nz * block, slots), x, preferred_element_type=F32)
            acc[f] = own.reshape(nz, block, fc)
            weight = wt[:, columns(f)]
            y = jnp.dot(hid[...], weight, preferred_element_type=F32)
            eo[f] = y.astype(BF16).reshape(ne, cap, fc)
            for d in range(1, ne):
                e = lax.rem(me + d, ne)
                eo_copy(f, d, e, me).start()
            ret[f, me] = eo[f, me]
            core_copy(f).wait_recv()
            acc[f] += crecv[f].astype(F32)

        for k in range(nz):
            up = s - k

            @pl.when((z == k) & (up >= 0) & (up < nf))
            def _():
                for zz in range(nz - 1, k, -1):
                    term = acc[up, zz]
                    if k > 0:
                        up_copy(up, zz).wait_recv()
                        term += rrecv[up, zz].astype(F32)
                    rsend[up, zz] = term.astype(BF16)
                    up_copy(up, zz).start()

            down = s - (nz - 1 - k)

            @pl.when((z == k) & (down >= 0) & (down < nf))
            def _():
                for zz in range(k):
                    term = acc[down, zz]
                    if k < nz - 1:
                        down_copy(down, zz).wait_recv()
                        term += lrecv[down, zz].astype(F32)
                    lsend[down, zz] = term.astype(BF16)
                    down_copy(down, zz).start()

        @pl.when(s < nf)
        def _():
            hgacc[...] += lax.dot_general(
                inc[s].reshape(slots, fc), wt[:, columns(s)],
                (((1,), (1,)), ((), ())), preferred_element_type=F32)

        back = s - (nz - 1)

        @pl.when(back >= 0)
        def _():
            f = back
            for d in range(1, ne):
                e = lax.rem(me + ne - d, ne)
                eo_copy(f, d, e, e).wait_recv()
            grads = og[:, columns(f)].astype(F32)
            mixed = jnp.zeros((tok, fc), F32)
            for e in range(ne):
                routed = jnp.dot(sel_t[e], ret[f, e], preferred_element_type=F32)
                mixed += gcol[e] * routed
                product = routed * grads
                part = product[:, 0:128]
                for j in range(128, fc, 128):
                    part += product[:, j:j + 128]
                qacc[e] += part
            mixed_ref[:, columns(f)] = mixed.astype(BF16)

            wg_ref[:, columns(f)] = acc[f, z]

            @pl.when(z > 0)
            def _():
                up_copy(f, z).wait_recv()
                wg_ref[:, columns(f)] += rrecv[f, z].astype(F32)

            @pl.when(z < nz - 1)
            def _():
                down_copy(f, z).wait_recv()
                wg_ref[:, columns(f)] += lrecv[f, z].astype(F32)

    hg_ref[...] = hgacc[...].astype(BF16)
    sums = [to_row(jnp.sum(qacc[e], axis=1, keepdims=True)) for e in range(ne)]
    for k in range(top):
        total = jnp.zeros((1, tok), F32)
        for e in range(ne):
            total += jnp.where(ids[k:k + 1, :] == e, sums[e], 0.0)
        gate_ref[k:k + 1, :] = total

    @pl.loop(0, nf)
    def _(f):
        core_copy(f).wait_send()
        for d in range(1, ne):
            e = lax.rem(me + d, ne)
            cot_copy(f, d, e, me).wait_send()
            eo_copy(f, d, e, me).wait_send()
        for k in range(nz):
            @pl.when(z == k)
            def _():
                for zz in range(k + 1, nz):
                    up_copy(f, zz).wait_send()
                for zz in range(k):
                    down_copy(f, zz).wait_send()


def on_device(route_ids, gate_values, out_grad, down_weight, hidden):
    ne = lax.axis_size("expert")
    nz = lax.axis_size("dp") // 2
    cap, width = hidden.shape[3:]
    tok, feat = out_grad.shape
    top = route_ids.shape[1]
    nf = CHUNKS
    fc = feat // nf
    block = width // (2 * nz)
    slots = ne * cap
    chain = pltpu.VMEM((nf, nz, block, fc), BF16)
    dma = pltpu.SemaphoreType.DMA
    vmem = pl.BlockSpec(memory_space=pltpu.VMEM)
    out_shape = (
        jax.ShapeDtypeStruct((tok, feat), BF16),
        jax.ShapeDtypeStruct((top, tok), F32),
        jax.ShapeDtypeStruct((slots, width), BF16),
        jax.ShapeDtypeStruct((block, feat), F32),
    )
    hbm = pl.BlockSpec(memory_space=pltpu.HBM)
    mixed, gate, hg, wg = pl.pallas_call(
        functools.partial(fused_kernel, nf),
        out_shape=out_shape,
        in_specs=[vmem, vmem, hbm, hbm, hbm],
        out_specs=(vmem,) * 4,
        scratch_shapes=[
            pltpu.VMEM((tok, feat), BF16),
            pltpu.VMEM((width, feat), BF16),
            pltpu.VMEM((slots, width), BF16),
            pltpu.VMEM((width, slots), BF16),
            pltpu.VMEM((2, nz, block, slots), BF16),
            pltpu.VMEM((ne, cap, tok), BF16),
            pltpu.VMEM((ne, tok, cap), BF16),
            pltpu.VMEM((ne, cap, 1), F32),
            pltpu.VMEM((ne, tok, 1), F32),
            pltpu.VMEM((nf, ne - 1, cap, fc), BF16),
            pltpu.VMEM((nf, ne, cap, fc), BF16),
            pltpu.VMEM((nf, ne, cap, fc), BF16),
            pltpu.VMEM((nf, ne, cap, fc), BF16),
            chain,
            chain,
            pltpu.VMEM((nf, nz, block, fc), F32),
            chain,
            chain,
            chain,
            chain,
            pltpu.VMEM((slots, width), F32),
            pltpu.VMEM((ne, tok, 128), F32),
            dma((nf, ne - 1)),
            dma((nf, ne - 1)),
            dma((nf, ne - 1)),
            dma((nf, ne - 1)),
            dma((nf,)),
            dma((nf,)),
            dma((nf, nz)),
            dma((nf, nz)),
            dma((nf, nz)),
            dma((nf, nz)),
            dma((3,)),
        ],
        compiler_params=pltpu.CompilerParams(
            collective_id=0, has_side_effects=True, vmem_limit_bytes=52 * 1024 * 1024
        ),
        cost_estimate=pl.CostEstimate(
            flops=6 * slots * width * feat, bytes_accessed=2 * width * feat, transcendentals=0
        ),
    )(route_ids.T, gate_values.T, out_grad, down_weight[0], hidden.reshape(slots, width))
    return mixed, gate.T, hg.reshape(hidden.shape), wg[None]


def fits(mesh):
    return mesh.shape["expert"] <= 4 and mesh.shape["dp"] in (2, 4, 8)


def solution(mesh):
    in_specs = (
        P(("dp", "expert"), None),
        P(("dp", "expert"), None),
        P(("dp", "expert"), None),
        P("expert", None, None),
        P("dp", "expert", None, None, None),
    )
    out_specs = (
        P(("dp", "expert"), None),
        P(("dp", "expert"), None),
        P("dp", "expert", None, None, None),
        P("expert", "dp", None),
    )
    body = on_device if fits(mesh) else on_device_generic
    return jax.shard_map(
        body, mesh=mesh, in_specs=in_specs, out_specs=out_specs, check_vma=False
    )
```

```python
import functools

import jax
import jax.numpy as jnp
from jax import lax
from jax.experimental import pallas as pl
from jax.experimental.pallas import tpu as pltpu
from jax.sharding import PartitionSpec as P


MESH = pl.DeviceIdType.MESH
CHUNKS = 8
AHEAD = 2
F32 = jnp.float32
BF16 = jnp.bfloat16


def slot_table(route_ids, experts, capacity):
    flat_ids = route_ids.reshape(-1)
    route_count = flat_ids.shape[0]
    onehot = (flat_ids[:, None] == jnp.arange(experts, dtype=jnp.int32)[None, :]).astype(
        jnp.float32
    )
    positions = jnp.arange(route_count, dtype=jnp.int32)
    earlier = (positions[:, None] > positions[None, :]).astype(jnp.float32)
    before = jnp.dot(
        earlier, onehot, precision=lax.Precision.HIGHEST, preferred_element_type=jnp.float32
    )
    slot_rank = jnp.sum(before * onehot, axis=1).astype(jnp.int32)
    slot_index = flat_ids * capacity + slot_rank
    slots_all = jnp.arange(experts * capacity, dtype=jnp.int32)
    return (slots_all[:, None] == slot_index[None, :]).astype(jnp.bfloat16)


def on_device_generic(route_ids, gate_values, out_grad, down_weight, hidden):
    experts = lax.axis_size("expert")
    capacity = hidden.shape[3]
    inner_width = hidden.shape[4]
    feature_width = out_grad.shape[1]
    tok_rows = route_ids.shape[0]
    routes = route_ids.shape[1]
    slot_map = slot_table(route_ids, experts, capacity)
    weight_mat = down_weight[0]
    rows_in = hidden.reshape(-1, inner_width)
    expert_out = jnp.dot(rows_in, weight_mat, preferred_element_type=jnp.float32)
    expert_out = expert_out.astype(jnp.bfloat16).reshape(experts, capacity, feature_width)
    grads_f = out_grad.astype(jnp.float32)
    scaled = (
        (gate_values[:, :, None] * grads_f[:, None, :])
        .reshape(-1, feature_width)
        .astype(jnp.bfloat16)
    )
    outgoing = jnp.dot(slot_map, scaled, preferred_element_type=jnp.float32)
    outgoing = outgoing.astype(jnp.bfloat16).reshape(experts, capacity, feature_width)
    returned = lax.all_to_all(expert_out, "expert", split_axis=0, concat_axis=0, tiled=True)
    incoming = lax.all_to_all(outgoing, "expert", split_axis=0, concat_axis=0, tiled=True)
    gathered = jnp.einsum(
        "sr,sd->rd",
        slot_map,
        returned.reshape(-1, feature_width),
        preferred_element_type=jnp.float32,
    )
    gathered = gathered.reshape(tok_rows, routes, feature_width)
    mixed_out = jnp.sum(gate_values[:, :, None] * gathered, axis=1).astype(jnp.bfloat16)
    gate_grad = jnp.sum(gathered * grads_f[:, None, :], axis=2)
    grad_rows = incoming.reshape(-1, feature_width)
    hidden_grad = jnp.einsum("sd,hd->sh", grad_rows, weight_mat, preferred_element_type=jnp.float32)
    hidden_grad = hidden_grad.astype(jnp.bfloat16).reshape(hidden.shape)
    partial_term = jnp.einsum("sh,sd->hd", rows_in, grad_rows, preferred_element_type=jnp.float32)
    weight_grad = lax.psum_scatter(partial_term, "dp", scatter_dimension=0, tiled=True)
    return (mixed_out, gate_grad, hidden_grad, weight_grad[None])


def fused_kernel(
    nf, ids_ref, gates_ref, og_hbm, w_hbm, hid_hbm,
    mixed_ref, gate_ref, hg_ref, wg_ref,
    og, wt, hid, hall, ht, sel, sel_t, gslot, gcol, outg, inc, eo, ret, csend, crecv, acc,
    rsend, rrecv, lsend, lrecv, hgacc, qacc,
    cot_s, cot_r, eo_s, eo_r, core_s, core_r, rs, rr, ls, lr, load,
):
    dp, me = lax.axis_index("dp"), lax.axis_index("expert")
    ne = lax.axis_size("expert")
    nz = lax.axis_size("dp") // 2
    z, core = lax.div(dp, 2), lax.rem(dp, 2)
    top, tok = ids_ref.shape
    cap = inc.shape[2]
    fc = inc.shape[3]
    block = wg_ref.shape[0]
    slots = ne * cap
    mate = 2 * z + 1 - core

    loads = [
        pltpu.make_async_copy(src, dst, load.at[i])
        for i, (src, dst) in enumerate(((og_hbm, og), (hid_hbm, hid), (w_hbm, wt)))
    ]
    for copy in loads:
        copy.start()

    barrier = pltpu.get_barrier_semaphore()
    for d in range(1, ne):
        pl.semaphore_signal(barrier, inc=1, device_id=(dp, lax.rem(me + d, ne)), device_id_type=MESH)
    pl.semaphore_signal(barrier, inc=1, device_id=(mate, me), device_id_type=MESH)

    @pl.when(z > 0)
    def _():
        pl.semaphore_signal(barrier, inc=1, device_id=(dp - 2, me), device_id_type=MESH)

    @pl.when(z < nz - 1)
    def _():
        pl.semaphore_signal(barrier, inc=1, device_id=(dp + 2, me), device_id_type=MESH)

    ids = ids_ref[...]
    gates = gates_ref[...]
    row = lax.broadcasted_iota(jnp.int32, (tok, tok), 0)
    col = lax.broadcasted_iota(jnp.int32, (tok, tok), 1)
    diagonal = row == col
    earlier = row < col
    slot_rows = lax.broadcasted_iota(jnp.int32, (cap, tok), 0).astype(F32)
    slot_cols = lax.broadcasted_iota(jnp.int32, (tok, cap), 1).astype(F32)

    def to_column(values):
        return jnp.sum(jnp.where(diagonal, values, 0.0), axis=1, keepdims=True)

    def to_row(values):
        return jnp.sum(jnp.where(diagonal, values, 0.0), axis=0, keepdims=True)

    for e in range(ne):
        named = jnp.sum(jnp.where(ids == e, 1.0, 0.0), axis=0, keepdims=True)
        gate = jnp.sum(jnp.where(ids == e, gates, 0.0), axis=0, keepdims=True)
        rank = jnp.sum(jnp.where(earlier, to_column(named), 0.0), axis=0, keepdims=True)
        place = jnp.where(named > 0.0, rank, -1.0)
        hit = slot_rows == place
        sel[e] = jnp.where(hit, 1.0, 0.0).astype(BF16)
        gslot[e] = jnp.sum(jnp.where(hit, gate, 0.0), axis=1, keepdims=True)
        sel_t[e] = jnp.where(slot_cols == to_column(place), 1.0, 0.0).astype(BF16)
        gcol[e] = to_column(gate)

    count = ne + jnp.where(z > 0, 1, 0) + jnp.where(z < nz - 1, 1, 0)
    pl.semaphore_wait(barrier, count)

    def columns(f):
        return pl.ds(pl.multiple_of(f * fc, fc), fc)

    def cot_copy(f, d, peer, slot):
        return pltpu.make_async_remote_copy(
            src_ref=outg.at[f, d - 1], dst_ref=inc.at[f, slot],
            send_sem=cot_s.at[f, d - 1], recv_sem=cot_r.at[f, d - 1],
            device_id=(dp, peer), device_id_type=MESH)

    def eo_copy(f, d, peer, slot):
        return pltpu.make_async_remote_copy(
            src_ref=eo.at[f, peer], dst_ref=ret.at[f, slot],
            send_sem=eo_s.at[f, d - 1], recv_sem=eo_r.at[f, d - 1],
            device_id=(dp, peer), device_id_type=MESH)

    def core_copy(f):
        return pltpu.make_async_remote_copy(
            src_ref=csend.at[f], dst_ref=crecv.at[f],
            send_sem=core_s.at[f], recv_sem=core_r.at[f],
            device_id=(mate, me), device_id_type=MESH)

    def up_copy(f, k):
        return pltpu.make_async_remote_copy(
            src_ref=rsend.at[f, k], dst_ref=rrecv.at[f, k],
            send_sem=rs.at[f, k], recv_sem=rr.at[f, k],
            device_id=(lax.rem(dp + 2, 2 * nz), me), device_id_type=MESH)

    def down_copy(f, k):
        return pltpu.make_async_remote_copy(
            src_ref=lsend.at[f, k], dst_ref=lrecv.at[f, k],
            send_sem=ls.at[f, k], recv_sem=lr.at[f, k],
            device_id=(lax.rem(dp + 2 * nz - 2, 2 * nz), me), device_id_type=MESH)

    def send_cotangents(f):
        grads = og[:, columns(f)]
        for d in (*range(1, ne), 0):
            e = lax.rem(me + d, ne)
            rows = jnp.dot(sel[e], grads, preferred_element_type=F32)
            rows = (gslot[e] * rows).astype(BF16)
            if d:
                outg[f, d - 1] = rows
                cot_copy(f, d, e, me).start()
            else:
                inc[f, me] = rows

    loads[0].wait()

    @pl.loop(0, AHEAD)
    def _(f):
        send_cotangents(f)

    loads[1].wait()
    hall[...] = hid[...].T
    for zz in range(nz):
        ht[0, zz] = hall[pl.ds(pl.multiple_of(block * (2 * zz + 1 - core), block), block), :]
        ht[1, zz] = hall[pl.ds(pl.multiple_of(block * (2 * zz + core), block), block), :]
    loads[2].wait()
    hgacc[...] = jnp.zeros_like(hgacc)
    qacc[...] = jnp.zeros_like(qacc)

    @pl.loop(0, nf + nz - 1)
    def _(s):
        @pl.when(s < nf)
        def _():
            f = s

            @pl.when(f + AHEAD < nf)
            def _():
                send_cotangents(f + AHEAD)

            for d in range(1, ne):
                e = lax.rem(me + ne - d, ne)
                cot_copy(f, d, e, e).wait_recv()
            x = inc[f].reshape(slots, fc)
            other = jnp.dot(ht[0].reshape(nz * block, slots), x, preferred_element_type=F32)
            csend[f] = other.astype(BF16).reshape(nz, block, fc)
            core_copy(f).start()
            own = jnp.dot(ht[1].reshape(nz * block, slots), x, preferred_element_type=F32)
            acc[f] = own.reshape(nz, block, fc)
            weight = wt[:, columns(f)]
            y = jnp.dot(hid[...], weight, preferred_element_type=F32)
            eo[f] = y.astype(BF16).reshape(ne, cap, fc)
            for d in range(1, ne):
                e = lax.rem(me + d, ne)
                eo_copy(f, d, e, me).start()
            ret[f, me] = eo[f, me]
            hgacc[...] += lax.dot_general(
                x, weight, (((1,), (1,)), ((), ())), preferred_element_type=F32)
            core_copy(f).wait_recv()
            acc[f] += crecv[f].astype(F32)

        for k in range(nz):
            up = s - k

            @pl.when((z == k) & (up >= 0) & (up < nf))
            def _():
                for zz in range(nz - 1, k, -1):
                    term = acc[up, zz]
                    if k > 0:
                        up_copy(up, zz).wait_recv()
                        term += rrecv[up, zz].astype(F32)
                    rsend[up, zz] = term.astype(BF16)
                    up_copy(up, zz).start()

            down = s - (nz - 1 - k)

            @pl.when((z == k) & (down >= 0) & (down < nf))
            def _():
                for zz in range(k):
                    term = acc[down, zz]
                    if k < nz - 1:
                        down_copy(down, zz).wait_recv()
                        term += lrecv[down, zz].astype(F32)
                    lsend[down, zz] = term.astype(BF16)
                    down_copy(down, zz).start()

        back = s - (nz - 1)

        @pl.when(back >= 0)
        def _():
            f = back
            for d in range(1, ne):
                e = lax.rem(me + ne - d, ne)
                eo_copy(f, d, e, e).wait_recv()
            grads = og[:, columns(f)].astype(F32)
            mixed = jnp.zeros((tok, fc), F32)
            for e in range(ne):
                routed = jnp.dot(sel_t[e], ret[f, e], preferred_element_type=F32)
                mixed += gcol[e] * routed
                product = routed * grads
                part = product[:, 0:128]
                for j in range(128, fc, 128):
                    part += product[:, j:j + 128]
                qacc[e] += part
            mixed_ref[:, columns(f)] = mixed.astype(BF16)

            wg_ref[:, columns(f)] = acc[f, z]

            @pl.when(z > 0)
            def _():
                up_copy(f, z).wait_recv()
                wg_ref[:, columns(f)] += rrecv[f, z].astype(F32)

            @pl.when(z < nz - 1)
            def _():
                down_copy(f, z).wait_recv()
                wg_ref[:, columns(f)] += lrecv[f, z].astype(F32)

    hg_ref[...] = hgacc[...].astype(BF16)
    sums = [to_row(jnp.sum(qacc[e], axis=1, keepdims=True)) for e in range(ne)]
    for k in range(top):
        total = jnp.zeros((1, tok), F32)
        for e in range(ne):
            total += jnp.where(ids[k:k + 1, :] == e, sums[e], 0.0)
        gate_ref[k:k + 1, :] = total

    @pl.loop(0, nf)
    def _(f):
        core_copy(f).wait_send()
        for d in range(1, ne):
            e = lax.rem(me + d, ne)
            cot_copy(f, d, e, me).wait_send()
            eo_copy(f, d, e, me).wait_send()
        for k in range(nz):
            @pl.when(z == k)
            def _():
                for zz in range(k + 1, nz):
                    up_copy(f, zz).wait_send()
                for zz in range(k):
                    down_copy(f, zz).wait_send()


def on_device(route_ids, gate_values, out_grad, down_weight, hidden):
    ne = lax.axis_size("expert")
    nz = lax.axis_size("dp") // 2
    cap, width = hidden.shape[3:]
    tok, feat = out_grad.shape
    top = route_ids.shape[1]
    nf = CHUNKS
    fc = feat // nf
    block = width // (2 * nz)
    slots = ne * cap
    chain = pltpu.VMEM((nf, nz, block, fc), BF16)
    dma = pltpu.SemaphoreType.DMA
    vmem = pl.BlockSpec(memory_space=pltpu.VMEM)
    out_shape = (
        jax.ShapeDtypeStruct((tok, feat), BF16),
        jax.ShapeDtypeStruct((top, tok), F32),
        jax.ShapeDtypeStruct((slots, width), BF16),
        jax.ShapeDtypeStruct((block, feat), F32),
    )
    hbm = pl.BlockSpec(memory_space=pltpu.HBM)
    mixed, gate, hg, wg = pl.pallas_call(
        functools.partial(fused_kernel, nf),
        out_shape=out_shape,
        in_specs=[vmem, vmem, hbm, hbm, hbm],
        out_specs=(vmem,) * 4,
        scratch_shapes=[
            pltpu.VMEM((tok, feat), BF16),
            pltpu.VMEM((width, feat), BF16),
            pltpu.VMEM((slots, width), BF16),
            pltpu.VMEM((width, slots), BF16),
            pltpu.VMEM((2, nz, block, slots), BF16),
            pltpu.VMEM((ne, cap, tok), BF16),
            pltpu.VMEM((ne, tok, cap), BF16),
            pltpu.VMEM((ne, cap, 1), F32),
            pltpu.VMEM((ne, tok, 1), F32),
            pltpu.VMEM((nf, ne - 1, cap, fc), BF16),
            pltpu.VMEM((nf, ne, cap, fc), BF16),
            pltpu.VMEM((nf, ne, cap, fc), BF16),
            pltpu.VMEM((nf, ne, cap, fc), BF16),
            chain,
            chain,
            pltpu.VMEM((nf, nz, block, fc), F32),
            chain,
            chain,
            chain,
            chain,
            pltpu.VMEM((slots, width), F32),
            pltpu.VMEM((ne, tok, 128), F32),
            dma((nf, ne - 1)),
            dma((nf, ne - 1)),
            dma((nf, ne - 1)),
            dma((nf, ne - 1)),
            dma((nf,)),
            dma((nf,)),
            dma((nf, nz)),
            dma((nf, nz)),
            dma((nf, nz)),
            dma((nf, nz)),
            dma((3,)),
        ],
        compiler_params=pltpu.CompilerParams(
            collective_id=0, has_side_effects=True, vmem_limit_bytes=52 * 1024 * 1024
        ),
        cost_estimate=pl.CostEstimate(
            flops=6 * slots * width * feat, bytes_accessed=2 * width * feat, transcendentals=0
        ),
    )(route_ids.T, gate_values.T, out_grad, down_weight[0], hidden.reshape(slots, width))
    return mixed, gate.T, hg.reshape(hidden.shape), wg[None]


def fits(mesh):
    return mesh.shape["expert"] <= 4 and mesh.shape["dp"] in (2, 4, 8)


def solution(mesh):
    in_specs = (
        P(("dp", "expert"), None),
        P(("dp", "expert"), None),
        P(("dp", "expert"), None),
        P("expert", None, None),
        P("dp", "expert", None, None, None),
    )
    out_specs = (
        P(("dp", "expert"), None),
        P(("dp", "expert"), None),
        P("dp", "expert", None, None, None),
        P("expert", "dp", None),
    )
    body = on_device if fits(mesh) else on_device_generic
    return jax.shard_map(
        body, mesh=mesh, in_specs=in_specs, out_specs=out_specs, check_vma=False
    )
```
